256 devices in a mesh: aux: 32 (over z, y), rep: 8 (over x, core).
Axes of the slice: x: 4, y: 4, z: 8, core: 2. Of those that a mesh axis runs over, the one named last changes fastest.
Arguments:
- basis_tensor: bfloat16 [1280, 384, 384], P('aux'), may hold values from -6 to 6
- aux_pattern: int32 [20, 6, 6], replicated, may hold values 0 or 1
- green_pattern: int32 [6, 6], replicated, may hold values 0 or 1
- green_occ: bfloat16 [384, 384], replicated, may hold values from -0.3125 to 0.3125
- green_vir: bfloat16 [384, 384], replicated, may hold values from -0.3125 to 0.3125
Outputs:
- chi: float32 [1280, 1280], P('aux', 'rep')
The draws below stay inside these ranges and needn't reach their ends.
All inputs are finite; a program needn't handle non-finite values.
Results may differ from the reference program's by a relative error of at most 0.0041.
Values may be sent and summed in bfloat16 or wider, within the bound.
No kernel may reach another device: no remote copies, remote signals or barrier semaphores. Data moves between devices by JAX's collectives and lax.ppermute only.
A program may use at most 128 MiB of HBM per device.

```python
import jax
import jax.numpy as jnp
from jax import lax

BLOCK = 64
ABLOCK = 64
NB = 6
NAO = 384
NAUX = 1280


def plant(array, own_key, least, top_value):
    shape = array.shape
    index_at = [jax.random.randint(jax.random.fold_in(own_key, axis), (), 0, shape[axis]) for axis in range(len(shape))]
    array = array.at[tuple(index_at)].set(least)
    longest = shape.index(max(shape))
    index_at[longest] = (index_at[longest] + 1) % shape[longest]
    return array.at[tuple(index_at)].set(top_value)


def steps_of(stream_key, dims, pieces, low, largest):
    factor_of = 1.0
    for axis_at, shards_of in pieces:
        draws = jax.random.uniform(jax.random.fold_in(jax.random.fold_in(stream_key, 6), axis_at), (shards_of,), jnp.float32, low / len(pieces), largest / len(pieces))
        factor_of = factor_of * jnp.repeat(jnp.exp(draws), dims[axis_at] // shards_of).reshape((-1,) + (1,) * (len(dims) - 1 - axis_at))
    return factor_of


def bell_draw(own_key, shape, deviation, reach, shards=(), held_as=jnp.bfloat16):
    result = deviation * jax.random.normal(own_key, shape, jnp.float32)
    if shards:
        result = result * steps_of(own_key, shape, shards, -0.22, 0.18)
    return jnp.clip(result, -reach, reach).astype(held_as)


def setup_inputs(seed: int = 0) -> dict:
    arg_keys = jax.random.split(jax.random.key(seed), 6)
    return {
        "basis_tensor": bell_draw(arg_keys[0], (NAUX, NAO, NAO), 1.0, 6.0, ((0, 32),)),
        "aux_pattern": plant((jax.random.randint(arg_keys[1], (NAUX // ABLOCK, NB, NB), 0, 4) < 3).astype(jnp.int32), jax.random.fold_in(arg_keys[1], 1), 0, 1),
        "green_pattern": plant((jax.random.randint(arg_keys[2], (NB, NB), 0, 3) < 2).astype(jnp.int32), jax.random.fold_in(arg_keys[2], 1), 0, 1),
        "green_occ": bell_draw(arg_keys[3], (NAO, NAO), NAO ** -0.5, 0.3125),
        "green_vir": bell_draw(arg_keys[4], (NAO, NAO), NAO ** -0.5, 0.3125),
    }


def widen(pattern, size):
    return jnp.repeat(jnp.repeat(pattern, size, axis=-1), size, axis=-2)


def reference(basis_tensor, aux_pattern, green_pattern, green_occ, green_vir):
    green_mask = widen(green_pattern, BLOCK).astype(jnp.bfloat16)
    occ = green_occ * green_mask
    vir = green_vir * green_mask
    per_function = jnp.repeat(aux_pattern, ABLOCK, axis=0)

    def transform(pair):
        tile, pattern = pair
        masked = tile * widen(pattern, BLOCK).astype(jnp.bfloat16)
        first = jnp.dot(occ, masked, preferred_element_type=jnp.float32).astype(jnp.bfloat16)
        product = jnp.dot(first, vir, preferred_element_type=jnp.float32).astype(jnp.bfloat16)
        return masked, product

    masked, product = lax.map(transform, (basis_tensor, per_function))
    flat_masked = masked.reshape(NAUX, NAO * NAO)
    flat_product = product.reshape(NAUX, NAO * NAO)
    chi = lax.dot_general(flat_masked, flat_product, (((1,), (1,)), ((), ())), preferred_element_type=jnp.float32)
    return chi * (1.0 / NAO)
```

```python
import functools

import jax
import jax.numpy as jnp
from jax import lax
from jax.experimental import pallas as pl
from jax.experimental.pallas import tpu as pltpu
from jax.sharding import Mesh, PartitionSpec as P

BLOCK = 64
ABLOCK = 64
NZ, NY, NX, NC = 8, 4, 4, 2
NR = NX * NC
LA = 40
NAO = 384
ROWS = NAO // NR
SUB = ROWS // NZ
HALF = SUB * NAO // 2
NB = NAO // BLOCK
F32 = jnp.float32
BF16 = jnp.bfloat16
LIMIT = 56 * 1024 * 1024


def row_mask(read, width=NAO):
    lane = lax.broadcasted_iota(jnp.int32, (1, width), 1) // BLOCK
    out = jnp.zeros((1, width), F32)
    for n in range(NB):
        out = jnp.where(lane == n, read(n).astype(F32), out)
    return out


def emit_chunks(sc_ref, held, own_ref, plus_ref, minus_ref):
    z = sc_ref[1]
    for d in range(NZ):
        dest = lax.rem(z + d, NZ)
        for j in range(SUB):
            h = j // 3
            if d == 0:
                out_ref, place = own_ref, h
            elif d < 4:
                out_ref, place = plus_ref, 2 * (d - 1) + h
            elif d > 4:
                out_ref, place = minus_ref, 2 * (7 - d) + h
            else:
                out_ref, place = (plus_ref, minus_ref)[h], 6
            for t in range(NAO // 128):
                rows = held[t, pl.ds(dest * SUB + j, LA, stride=ROWS), :]
                out_ref[place, :, pl.ds((j % 3) * NAO + 128 * t, 128)] = rows.astype(BF16)


def prep_kernel(sc_ref, pat_ref, basis_ref, own_ref, plus_ref, minus_ref, held):
    r, place = sc_ref[0], sc_ref[2]
    for o in range(LA // 8):
        b = (place * LA + 8 * o) // ABLOCK
        for jo in range(ROWS // 8):
            mb = (r * ROWS + 8 * jo) // BLOCK
            mask = row_mask(lambda n: pat_ref[(b * NB + mb) * NB + n])
            for p in range(8 * o, 8 * o + 8):
                rows = basis_ref[p, pl.ds(8 * jo, 8), :].astype(F32) * mask
                for t in range(NAO // 128):
                    held[t, pl.ds(p * ROWS + 8 * jo, 8), :] = rows[:, 128 * t : 128 * t + 128]
    emit_chunks(sc_ref, held, own_ref, plus_ref, minus_ref)


CHUNKS = (
    jax.ShapeDtypeStruct((2, LA, HALF), BF16),
    jax.ShapeDtypeStruct((7, LA, HALF), BF16),
    jax.ShapeDtypeStruct((7, LA, HALF), BF16),
)
CHUNK_SPECS = tuple(pl.BlockSpec(s.shape, lambda *_: (0, 0, 0)) for s in CHUNKS)


def prep(sc, pat, basis):
    return pl.pallas_call(
        prep_kernel,
        out_shape=CHUNKS,
        grid_spec=pltpu.PrefetchScalarGridSpec(
            num_scalar_prefetch=2,
            grid=(1,),
            in_specs=[pl.BlockSpec((LA, ROWS, NAO), lambda i, sc, pat: (0, sc[0], 0))],
            out_specs=CHUNK_SPECS,
            scratch_shapes=[pltpu.VMEM((NAO // 128, LA * ROWS, 128), F32)],
        ),
        compiler_params=pltpu.CompilerParams(vmem_limit_bytes=LIMIT),
        cost_estimate=pl.CostEstimate(flops=10**6, bytes_accessed=3 * 10**6, transcendentals=0),
        name="prep",
    )(sc, pat, basis)


STEPQ = 8


def product_kernel(
    sc_ref, pat_ref, gpat_ref, basis_ref, occ_ref, vir_ref, own_ref, plus_ref, minus_ref,
    first, held, occ, vir, masks,
):
    i = pl.program_id(0)
    r, place = sc_ref[0], sc_ref[2]
    b0 = (place * LA) // ABLOCK
    nblocks = pat_ref.shape[0] // (NB * NB)

    @pl.when(i == 0)
    def _():
        for mb in range(NB):
            rows = pl.ds(mb * BLOCK, BLOCK)
            g = row_mask(lambda n: gpat_ref[mb * NB + n]).astype(BF16)
            vir[rows, :] = vir_ref[rows, :] * g
            for k in range(2):
                b = jnp.minimum(b0 + k, nblocks - 1)
                m = row_mask(lambda n: pat_ref[(b * NB + mb) * NB + n])
                masks[k, rows, :] = jnp.broadcast_to(m, (BLOCK, NAO)).astype(BF16)
        for jo in range(ROWS // 16):
            gb = (r * ROWS + 16 * jo) // BLOCK
            g = row_mask(lambda n: gpat_ref[gb * NB + n]).astype(BF16)
            rows = pl.ds(16 * jo, 16)
            occ[rows, :] = occ_ref[rows, :] * g

    which = (place * LA + STEPQ * i) // ABLOCK - b0
    mask = masks[which]
    rows_r = occ[...]
    for q in range(STEPQ):
        masked = basis_ref[q] * mask
        f = jnp.dot(rows_r, masked, preferred_element_type=F32).astype(BF16)
        first[pl.ds(pl.multiple_of((STEPQ * i + q) * ROWS, 16), ROWS), :] = f

    @pl.when(i == LA // STEPQ - 1)
    def _():
        v = vir[...]
        n = LA * ROWS // 4
        for t in range(4):
            part = jnp.dot(first[pl.ds(t * n, n), :], v, preferred_element_type=F32)
            for u in range(NAO // 128):
                held[u, pl.ds(t * n, n), :] = part[:, 128 * u : 128 * u + 128]
        emit_chunks(sc_ref, held, own_ref, plus_ref, minus_ref)


def products(sc, pat, gpat, basis, occ, vir):
    return pl.pallas_call(
        product_kernel,
        out_shape=CHUNKS,
        grid_spec=pltpu.PrefetchScalarGridSpec(
            num_scalar_prefetch=3,
            grid=(LA // STEPQ,),
            in_specs=[
                pl.BlockSpec((STEPQ, NAO, NAO), lambda i, *_: (i, 0, 0)),
                pl.BlockSpec((ROWS, NAO), lambda i, sc, pat, gpat: (sc[0], 0)),
                pl.BlockSpec((NAO, NAO), lambda i, *_: (0, 0)),
            ],
            out_specs=CHUNK_SPECS,
            scratch_shapes=[
                pltpu.VMEM((LA * ROWS, NAO), BF16),
                pltpu.VMEM((NAO // 128, LA * ROWS, 128), F32),
                pltpu.VMEM((ROWS, NAO), BF16),
                pltpu.VMEM((NAO, NAO), BF16),
                pltpu.VMEM((2, NAO, NAO), BF16),
            ],
        ),
        compiler_params=pltpu.CompilerParams(vmem_limit_bytes=LIMIT),
        cost_estimate=pl.CostEstimate(
            flops=4 * LA * ROWS * NAO * NAO, bytes_accessed=14 * 10**6, transcendentals=0
        ),
        name="products",
    )(sc, pat, gpat, basis, occ, vir)


def shift(value, by, axis, n):
    return lax.ppermute(value, axis, [(i, (i + by) % n) for i in range(n)])


def along_z(own, plus, minus):
    got = {(0, 0): (own, 0), (0, 1): (own, 1)}
    for t in range(1, 5):
        plus, minus = shift(plus, 1, "z", NZ), shift(minus, -1, "z", NZ)
        if t < 4:
            for h in range(2):
                got[t, h] = (plus, h)
                got[8 - t, h] = (minus, h)
            plus, minus = plus[2:], minus[2:]
        else:
            got[4, 0] = (plus, 0)
            got[4, 1] = (minus, 0)
    return got


GROUPS = (
    ((0, 0), (0, 1), (1, 0), (1, 1), (7, 0), (7, 1)),
    ((2, 0), (2, 1), (6, 0), (6, 1), (3, 0), (3, 1), (5, 0), (5, 1), (4, 0), (4, 1)),
)


def along_y(got):
    out = {}
    for keys in GROUPS:
        group = jnp.concatenate([got[k][0][got[k][1]][None] for k in keys], axis=0)
        n = len(keys) // 2
        below, above = shift(group, 1, "y", NY), shift(group, -1, "y", NY)
        far = shift(below[:n], 1, "y", NY), shift(above[n:], -1, "y", NY)
        for i, (d, h) in enumerate(keys):
            out[d, 0, h] = (group, i)
            out[d, 1, h] = (below, i)
            out[d, 3, h] = (above, i)
            out[d, 2, h] = (far[i // n], i % n)
    return out


TILE = 256


def contract_kernel(m_places, p_places, n_arrays, sc_ref, *refs):
    arrays, (keep_ref, send_ref, left, right) = refs[:n_arrays], refs[n_arrays:]
    z, c = sc_ref[1], sc_ref[3]
    first_even = lax.rem(z + c, 2) == 0
    for (d, h), (a, i) in p_places.items():
        left[h, pl.ds(d * LA, LA), :] = arrays[a][i]
    for (d, e, h), (a, i) in m_places.items():
        right[h, pl.ds((d * NY + e) * LA, LA), :] = arrays[a][i]

    @pl.loop(0, NZ * NY * LA // TILE)
    def _(t):
        cols = pl.ds(pl.multiple_of(t * TILE, TILE), TILE)
        acc = jnp.zeros((NZ * LA, TILE), F32)
        for h in range(2):
            acc += lax.dot_general(
                left[h], right[h, cols, :], (((1,), (1,)), ((), ())), preferred_element_type=F32
            )
        acc = acc.reshape(NZ // 2, 2, LA, TILE)
        keep_ref[:, :, cols] = jnp.where(first_even, acc[:, 0], acc[:, 1])
        send_ref[:, :, cols] = jnp.where(first_even, acc[:, 1], acc[:, 0])


def contract(sc, m, p):
    arrays, index = [], {}

    def places(table):
        out = {}
        for key, (array, i) in table.items():
            if id(array) not in index:
                index[id(array)] = len(arrays)
                arrays.append(array)
            out[key] = (index[id(array)], i)
        return out

    m_places, p_places = places(m), places(p)
    shape = jax.ShapeDtypeStruct((NZ // 2, LA, NZ * NY * LA), F32)
    return pl.pallas_call(
        functools.partial(contract_kernel, m_places, p_places, len(arrays)),
        out_shape=(shape, shape),
        in_specs=[pl.BlockSpec(memory_space=pltpu.SMEM)]
        + [pl.BlockSpec(memory_space=pltpu.VMEM)] * len(arrays),
        out_specs=(pl.BlockSpec(memory_space=pltpu.VMEM),) * 2,
        scratch_shapes=[
            pltpu.VMEM((2, NZ * LA, HALF), BF16),
            pltpu.VMEM((2, NZ * NY * LA, HALF), BF16),
        ],
        compiler_params=pltpu.CompilerParams(vmem_limit_bytes=LIMIT),
        cost_estimate=pl.CostEstimate(
            flops=4 * 320 * 1280 * 1152, bytes_accessed=10**7, transcendentals=0
        ),
        name="contract",
    )(sc, *arrays)


def pair_kernel(sc_ref, a_ref, b_ref, out_ref):
    out_ref[...] = a_ref[...] + b_ref[...]


def pair_sum(sc, keep, recv):
    block = (1,) + keep.shape[1:]

    def source(i, sc):
        first = lax.rem(sc[1] + sc[3], 2)
        return (lax.rem((sc[1] - first - sc[3]) // 2 - i + 8, NX), 0, 0)

    return pl.pallas_call(
        pair_kernel,
        out_shape=jax.ShapeDtypeStruct(keep.shape, F32),
        grid_spec=pltpu.PrefetchScalarGridSpec(
            num_scalar_prefetch=1,
            grid=(NX,),
            in_specs=[pl.BlockSpec(block, source)] * 2,
            out_specs=pl.BlockSpec(block, lambda i, sc: (i, 0, 0)),
        ),
        name="pair_sum",
    )(sc, keep, recv)


def pack_kernel(sc_ref, in_ref, out_ref):
    z, y = sc_ref[1], sc_ref[4]
    total = (in_ref[0] + in_ref[1]) + (in_ref[2] + in_ref[3])
    for d in range(NZ):
        for e in range(NY):
            k = d * NY + e
            part = total[:, k * LA : (k + 1) * LA]
            oct8 = [part[8 * o : 8 * o + 8] for o in range(5)]
            fill = jnp.zeros((8, 8), F32)
            upper = jnp.concatenate([oct8[0], oct8[1], oct8[2], fill], axis=1)
            lower = jnp.concatenate([oct8[3], oct8[4], jnp.zeros((8, 48), F32)], axis=1)
            dest = lax.rem(z - d + NZ, NZ) * NY + lax.rem(y - e + NY, NY)
            out_ref[dest, 0:8, :] = upper
            out_ref[dest, 8:16, :] = lower


def pack(sc, value):
    return pl.pallas_call(
        pack_kernel,
        out_shape=jax.ShapeDtypeStruct((NZ * NY, 16, 128), F32),
        in_specs=[
            pl.BlockSpec(memory_space=pltpu.SMEM),
            pl.BlockSpec(memory_space=pltpu.VMEM),
        ],
        out_specs=pl.BlockSpec(memory_space=pltpu.VMEM),
        name="pack",
    )(sc, value)


def finish_kernel(in_ref, out_ref):
    parts = []
    for y in range(NY):
        total = in_ref[y]
        for z in range(1, NZ):
            total = total + in_ref[z * NY + y]
        for o in range(5):
            lo = (o % 3) * LA
            parts.append(total[8 * (o // 3) : 8 * (o // 3) + 8, lo : lo + LA])
    rows = jnp.concatenate(parts, axis=0)
    rows = jnp.concatenate([rows, jnp.zeros((NY * LA, 128 - LA), F32)], axis=1)
    rows = jnp.concatenate([rows, jnp.zeros((256 - NY * LA, 128), F32)], axis=0)
    out_ref[...] = rows.T[:LA, : NY * LA] * (1.0 / NAO)


def finish(value):
    return pl.pallas_call(
        finish_kernel,
        out_shape=jax.ShapeDtypeStruct((LA, NY * LA), F32),
        in_specs=[pl.BlockSpec(memory_space=pltpu.VMEM)],
        out_specs=pl.BlockSpec(memory_space=pltpu.VMEM),
        name="finish",
    )(value)


def local(basis, aux_pattern, green_pattern, green_occ, green_vir):
    z, y, x, c = (lax.axis_index(a) for a in ("z", "y", "x", "core"))
    sc = jnp.stack([x * NC + c, z, z * NY + y, c, y, x]).astype(jnp.int32)
    pat, gpat = aux_pattern.reshape(-1), green_pattern.reshape(-1)
    m = along_y(along_z(*prep(sc, pat, basis)))
    p = along_z(*products(sc, pat, gpat, basis, green_occ, green_vir))
    keep, send = contract(sc, m, p)
    recv = shift(send, 1, "core", NC)
    by_x = lax.all_to_all(pair_sum(sc, keep, recv), "x", split_axis=0, concat_axis=0, tiled=True)
    by_zy = lax.all_to_all(pack(sc, by_x), ("z", "y"), split_axis=0, concat_axis=0, tiled=True)
    return finish(by_zy)


def solution(mesh):
    fine = Mesh(mesh.devices.reshape(NZ, NY, NX, NC), ("z", "y", "x", "core"))
    return jax.shard_map(
        local,
        mesh=fine,
        in_specs=(P(("z", "y"), None, None), P(), P(), P(), P()),
        out_specs=P(("z", "y"), ("x", "core")),
        check_vma=False,
    )
```

```python
import functools

import jax
import jax.numpy as jnp
from jax import lax
from jax.experimental import pallas as pl
from jax.experimental.pallas import tpu as pltpu
from jax.sharding import Mesh, PartitionSpec as P

BLOCK = 64
ABLOCK = 64
NZ, NY, NX, NC = 8, 4, 4, 2
NR = NX * NC
LA = 40
NAO = 384
LANES = 128
ROWS = NAO // NR
SUB = ROWS // NZ
FULL = SUB * NAO
HALF = FULL // 2
NB = NAO // BLOCK
F32 = jnp.float32
BF16 = jnp.bfloat16
MIB = 1024 * 1024


def places():
    z, y, x, c = (lax.axis_index(a) for a in ("z", "y", "x", "core"))
    return z, y, x * NC + c


def row_mask(read):
    lane = lax.broadcasted_iota(jnp.int32, (1, NAO), 1) // BLOCK
    out = jnp.zeros((1, NAO), F32)
    for n in range(NB):
        out = jnp.where(lane == n, read(n).astype(F32), out)
    return out


def emit(z, held, own_ref, plus_ref, minus_ref):
    for d in range(NZ):
        dest = lax.rem(z + d, NZ)
        for j in range(SUB):
            h = j // 3
            if d == 0:
                out_ref, place = own_ref, h
            elif d < 4:
                out_ref, place = plus_ref, 2 * (d - 1) + h
            elif d > 4:
                out_ref, place = minus_ref, 2 * (7 - d) + h
            else:
                out_ref, place = (plus_ref, minus_ref)[h], 6
            for t in range(NAO // LANES):
                rows = held[t, pl.ds(dest * SUB + j, LA, stride=ROWS), :]
                out_ref[place, :, pl.ds((j % 3) * NAO + LANES * t, LANES)] = rows.astype(BF16)


CHUNKS = tuple(jax.ShapeDtypeStruct((n, LA, HALF), BF16) for n in (2, 7, 7))


def prep_kernel(pat_ref, basis_ref, own_ref, plus_ref, minus_ref, slab, held, sems):
    z, y, r = places()
    place = z * NY + y
    steps = LA // 8
    start = pl.multiple_of(r * ROWS, 16)
    copies = [
        pltpu.make_async_copy(
            basis_ref.at[pl.ds(8 * o, 8), pl.ds(start, ROWS), :], slab.at[pl.ds(8 * o, 8)], sems.at[o]
        )
        for o in range(steps)
    ]
    for copy in copies:
        copy.start()
    for o in range(steps):
        b = (place * LA + 8 * o) // ABLOCK
        masks = [
            row_mask(lambda n: pat_ref[(r * ROWS + 8 * jo) // BLOCK, n, b]) for jo in range(ROWS // 8)
        ]
        copies[o].wait()
        for jo in range(ROWS // 8):
            for p in range(8 * o, 8 * o + 8):
                rows = slab[p, pl.ds(8 * jo, 8), :].astype(F32) * masks[jo]
                for t in range(NAO // LANES):
                    held[t, pl.ds(p * ROWS + 8 * jo, 8), :] = rows[:, LANES * t : LANES * (t + 1)]
    emit(z, held, own_ref, plus_ref, minus_ref)


SMEM = pl.BlockSpec(memory_space=pltpu.SMEM)
VMEM = pl.BlockSpec(memory_space=pltpu.VMEM)
HBM = pl.BlockSpec(memory_space=pltpu.HBM)
ANY = pl.BlockSpec(memory_space=pl.ANY)


def prep(pat, basis):
    return pl.pallas_call(
        prep_kernel,
        out_shape=CHUNKS,
        in_specs=[SMEM, HBM],
        out_specs=(VMEM, VMEM, VMEM),
        scratch_shapes=[
            pltpu.VMEM((LA, ROWS, NAO), BF16),
            pltpu.VMEM((NAO // LANES, LA * ROWS, LANES), F32),
            pltpu.SemaphoreType.DMA((LA // 8,)),
        ],
        compiler_params=pltpu.CompilerParams(vmem_limit_bytes=56 * MIB),
        cost_estimate=pl.CostEstimate(flops=10**6, bytes_accessed=3 * 10**6, transcendentals=0),
        name="prep",
    )(pat, basis)


STEPQ = 8


def product_kernel(
    pat_ref, gpat_ref, basis_ref, occ_ref, vir_ref, own_ref, plus_ref, minus_ref, first, held, occ, vir, masks
):
    i = pl.program_id(0)
    z, y, r = places()
    place = z * NY + y
    b0 = (place * LA) // ABLOCK
    nblocks = pat_ref.shape[2]

    @pl.when(i == 0)
    def _():
        for mb in range(NB):
            rows = pl.ds(mb * BLOCK, BLOCK)
            g = row_mask(lambda n: gpat_ref[mb, n]).astype(BF16)
            vir[rows, :] = vir_ref[rows, :] * g
            for k in range(2):
                b = jnp.minimum(b0 + k, nblocks - 1)
                m = row_mask(lambda n: pat_ref[mb, n, b])
                masks[k, rows, :] = jnp.broadcast_to(m, (BLOCK, NAO)).astype(BF16)
        for jo in range(ROWS // 16):
            start = pl.multiple_of(r * ROWS + 16 * jo, 16)
            g = row_mask(lambda n: gpat_ref[start // BLOCK, n]).astype(BF16)
            occ[pl.ds(16 * jo, 16), :] = occ_ref[pl.ds(start, 16), :] * g

    which = (place * LA + STEPQ * i) // ABLOCK - b0
    mask = masks[which]
    rows_r = occ[...]
    for q in range(STEPQ):
        masked = basis_ref[q] * mask
        f = jnp.dot(rows_r, masked, preferred_element_type=F32).astype(BF16)
        first[pl.ds(pl.multiple_of((STEPQ * i + q) * ROWS, 16), ROWS), :] = f

    @pl.when(i == LA // STEPQ - 1)
    def _():
        v = vir[...]
        n = LA * ROWS // 4
        for t in range(4):
            part = jnp.dot(first[pl.ds(t * n, n), :], v, preferred_element_type=F32)
            for u in range(NAO // LANES):
                held[u, pl.ds(t * n, n), :] = part[:, LANES * u : LANES * (u + 1)]
        emit(z, held, own_ref, plus_ref, minus_ref)


def products(pat, gpat, basis, occ, vir):
    return pl.pallas_call(
        product_kernel,
        out_shape=CHUNKS,
        grid=(LA // STEPQ,),
        in_specs=[
            SMEM,
            SMEM,
            pl.BlockSpec((STEPQ, NAO, NAO), lambda i: (i, 0, 0)),
            pl.BlockSpec((NAO, NAO), lambda i: (0, 0)),
            pl.BlockSpec((NAO, NAO), lambda i: (0, 0)),
        ],
        out_specs=tuple(pl.BlockSpec(c.shape, lambda i: (0, 0, 0)) for c in CHUNKS),
        scratch_shapes=[
            pltpu.VMEM((LA * ROWS, NAO), BF16),
            pltpu.VMEM((NAO // LANES, LA * ROWS, LANES), F32),
            pltpu.VMEM((ROWS, NAO), BF16),
            pltpu.VMEM((NAO, NAO), BF16),
            pltpu.VMEM((2, NAO, NAO), BF16),
        ],
        compiler_params=pltpu.CompilerParams(vmem_limit_bytes=56 * MIB),
        cost_estimate=pl.CostEstimate(
            flops=4 * LA * ROWS * NAO * NAO, bytes_accessed=14 * 10**6, transcendentals=0
        ),
        name="products",
    )(pat, gpat, basis, occ, vir)


def shift(value, by, axis, n):
    return lax.ppermute(value, axis, [(i, (i + by) % n) for i in range(n)])


def after(value, *others):
    return lax.optimization_barrier((value,) + others)[0]


GROUPS = ((0, 1, 7), (2, 6), (3, 5, 4))
EORDER = (0, 1, 3, 2)


def both(plus, minus, hops=1):
    return shift(plus, hops, "z", NZ), shift(minus, -hops, "z", NZ)


def round_y(group):
    return shift(group, 1, "y", NY), shift(group, -1, "y", NY)


def far_y(below, above):
    n = below.shape[0] // 2
    return shift(below[:n], 1, "y", NY), shift(above[n:], -1, "y", NY)


tie = lax.optimization_barrier


def spread(chunks, products_of):
    own, plus, minus = chunks
    p1, m1 = both(plus, minus)
    pown, pplus, pminus = products_of()
    n1 = jnp.concatenate([own, p1[:2], m1[:2]], axis=0)
    p1r, m1r, n1, pplus, pminus = tie((p1[2:], m1[2:], n1, pplus, pminus))
    p2, m2 = both(p1r, m1r)
    b1, a1 = round_y(n1)
    b1, a1, pplus, pminus = tie((b1, a1, pplus, pminus))
    p3, m3 = both(p2[2:4], m2[2:4])
    p4, m4 = both(p2[4:], m2[4:], 2)
    n2 = jnp.concatenate([p2[:2], m2[:2]], axis=0)
    b2, a2 = round_y(n2)
    f1 = far_y(b1, a1)
    q1, r1 = both(pplus, pminus)
    n3 = jnp.concatenate([p3, m3, p4, m4], axis=0)
    b3, a3 = round_y(n3)
    f2 = far_y(b2, a2)
    q2, r2 = both(q1[2:], r1[2:])
    b3, a3, q2, r2 = tie((b3, a3, q2, r2))
    f3 = far_y(b3, a3)
    q3, r3 = both(q2[2:4], r2[2:4])
    q4, r4 = both(q2[4:], r2[4:], 2)
    m = [n1, b1, a1, *f1, n2, b2, a2, *f2, n3, b3, a3, *f3]
    return m, [pown, q1, q2, q3, q4, r4, r3, r2, r1]


ORDER = [(d, e) for group in GROUPS for e in EORDER for d in group]


TILE = 256


def contract_kernel(np_, *refs):
    products_, arrays, (out_ref, left, right) = refs[:np_], refs[np_:-3], refs[-3:]
    z = lax.axis_index("z")
    at = 0
    for a in products_:
        for i in range(min(a.shape[0], 2)):
            left[at % 2, pl.ds(at // 2 * LA, LA), :] = a[i]
            at += 1
    at = 0
    for a in arrays:
        for i in range(a.shape[0]):
            right[at % 2, pl.ds(at // 2 * LA, LA), :] = a[i]
            at += 1
    for t in range(NZ * NY * LA // TILE):
        cols = pl.ds(t * TILE, TILE)
        acc = jnp.zeros((NZ * LA, TILE), F32)
        for h in range(2):
            acc += lax.dot_general(
                left[h], right[h, cols, :], (((1,), (1,)), ((), ())), preferred_element_type=F32
            )
        part = acc.reshape(NZ, LA, TILE).astype(BF16)
        for d in range(NZ):
            out_ref[lax.rem(z - d + NZ, NZ), :, cols] = part[d]


def contract(m, p):
    return pl.pallas_call(
        functools.partial(contract_kernel, len(p)),
        out_shape=jax.ShapeDtypeStruct((NZ, LA, NZ * NY * LA), BF16),
        in_specs=[VMEM] * (len(p) + len(m)),
        out_specs=VMEM,
        scratch_shapes=[
            pltpu.VMEM((2, NZ * LA, HALF), BF16),
            pltpu.VMEM((2, NZ * NY * LA, HALF), BF16),
        ],
        compiler_params=pltpu.CompilerParams(vmem_limit_bytes=24 * MIB),
        cost_estimate=pl.CostEstimate(
            flops=4 * 320 * 1280 * 1152, bytes_accessed=10**7, transcendentals=0
        ),
        name="contract",
    )(*p, *m)


def pack_kernel(in_ref, out_ref):
    z, y, _ = places()
    total = in_ref[0].astype(F32)
    for k in range(1, NR):
        total += in_ref[k].astype(F32)
    for k, (d, e) in enumerate(ORDER):
        part = total[:, k * LA : (k + 1) * LA]
        oct8 = [part[8 * o : 8 * o + 8] for o in range(5)]
        upper = jnp.concatenate([oct8[0], oct8[1], oct8[2], jnp.zeros((8, 8), F32)], axis=1)
        lower = jnp.concatenate([oct8[3], oct8[4], jnp.zeros((8, 48), F32)], axis=1)
        dest = lax.rem(z - d + NZ, NZ) * NY + lax.rem(y - e + NY, NY)
        out_ref[dest, 0:8, :] = upper
        out_ref[dest, 8:16, :] = lower


def pack(value):
    return pl.pallas_call(
        pack_kernel,
        out_shape=jax.ShapeDtypeStruct((NZ * NY, 16, LANES), F32),
        in_specs=[VMEM],
        out_specs=VMEM,
        name="pack",
    )(value)


def finish_kernel(in_ref, out_ref):
    parts = []
    for y in range(NY):
        total = in_ref[y]
        for z in range(1, NZ):
            total = total + in_ref[z * NY + y]
        for o in range(5):
            lo = (o % 3) * LA
            parts.append(total[8 * (o // 3) : 8 * (o // 3) + 8, lo : lo + LA])
    rows = jnp.concatenate(parts, axis=0)
    rows = jnp.concatenate([rows, jnp.zeros((NY * LA, LANES - LA), F32)], axis=1)
    rows = jnp.concatenate([rows, jnp.zeros((256 - NY * LA, LANES), F32)], axis=0)
    out_ref[...] = rows.T[:LA, : NY * LA] * (1.0 / NAO)


def finish(value):
    return pl.pallas_call(
        finish_kernel,
        out_shape=jax.ShapeDtypeStruct((LA, NY * LA), F32),
        in_specs=[VMEM],
        out_specs=VMEM,
        name="finish",
    )(value)


def local(basis, aux_pattern, green_pattern, green_occ, green_vir):
    pat = jnp.transpose(aux_pattern, (1, 2, 0))
    m, p = spread(
        prep(pat, basis), lambda: products(pat, green_pattern, basis, green_occ, green_vir)
    )
    parts = contract(m, p)
    by_rep = lax.all_to_all(parts, ("x", "core"), split_axis=0, concat_axis=0, tiled=True)
    by_zy = lax.all_to_all(pack(by_rep), ("z", "y"), split_axis=0, concat_axis=0, tiled=True)
    return finish(by_zy)


def solution(mesh):
    fine = Mesh(mesh.devices.reshape(NZ, NY, NX, NC), ("z", "y", "x", "core"))
    return jax.shard_map(
        local,
        mesh=fine,
        in_specs=(P(("z", "y"), None, None), P(), P(), P(), P()),
        out_specs=P(("z", "y"), ("x", "core")),
        check_vma=False,
    )
```

```python
import functools

import jax
import jax.numpy as jnp
from jax import lax
from jax.experimental import pallas as pl
from jax.experimental.pallas import tpu as pltpu
from jax.sharding import Mesh, PartitionSpec as P

BLOCK = 64
ABLOCK = 64
NZ, NY, NX, NC = 8, 4, 4, 2
NR = NX * NC
LA = 40
NAO = 384
LANES = 128
ROWS = NAO // NR
SUB = ROWS // NZ
FULL = SUB * NAO
HALF = FULL // 2
NB = NAO // BLOCK
F32 = jnp.float32
BF16 = jnp.bfloat16
MIB = 1024 * 1024


def places():
    z, y, x, c = (lax.axis_index(a) for a in ("z", "y", "x", "core"))
    return z, y, x * NC + c


def row_mask(read):
    lane = lax.broadcasted_iota(jnp.int32, (1, NAO), 1) // BLOCK
    out = jnp.zeros((1, NAO), F32)
    for n in range(NB):
        out = jnp.where(lane == n, read(n).astype(F32), out)
    return out


def emit(z, held, own_ref, plus_ref, minus_ref, *far_refs):
    for d in range(NZ):
        dest = lax.rem(z + d, NZ)
        for j in range(SUB):
            h = j // 3
            if d == 0:
                out_ref, place = own_ref, h
            elif d < 4:
                out_ref, place = plus_ref, 2 * (d - 1) + h
            elif d > 4:
                out_ref, place = minus_ref, 2 * (7 - d) + h
            else:
                out_ref, place = (far_refs[h], 0) if far_refs else ((plus_ref, minus_ref)[h], 6)
            for t in range(NAO // LANES):
                rows = held[t, pl.ds(dest * SUB + j, LA, stride=ROWS), :]
                out_ref[place, :, pl.ds((j % 3) * NAO + LANES * t, LANES)] = rows.astype(BF16)


CHUNKS = tuple(jax.ShapeDtypeStruct((n, LA, HALF), BF16) for n in (2, 6, 6, 1, 1))
WHOLE = tuple(jax.ShapeDtypeStruct((n, LA, HALF), BF16) for n in (2, 7, 7))


def prep_kernel(pat_ref, basis_ref, *refs):
    out_refs, (slab, held, sems) = refs[:-3], refs[-3:]
    z, y, r = places()
    place = z * NY + y
    steps = LA // 8
    start = pl.multiple_of(r * ROWS, 16)
    copies = [
        pltpu.make_async_copy(
            basis_ref.at[pl.ds(8 * o, 8), pl.ds(start, ROWS), :], slab.at[pl.ds(8 * o, 8)], sems.at[o]
        )
        for o in range(steps)
    ]
    for copy in copies:
        copy.start()
    for o in range(steps):
        b = (place * LA + 8 * o) // ABLOCK
        masks = [
            row_mask(lambda n: pat_ref[(r * ROWS + 8 * jo) // BLOCK, n, b]) for jo in range(ROWS // 8)
        ]
        copies[o].wait()
        for jo in range(ROWS // 8):
            for p in range(8 * o, 8 * o + 8):
                rows = slab[p, pl.ds(8 * jo, 8), :].astype(F32) * masks[jo]
                for t in range(NAO // LANES):
                    held[t, pl.ds(p * ROWS + 8 * jo, 8), :] = rows[:, LANES * t : LANES * (t + 1)]
    emit(z, held, *out_refs)


SMEM = pl.BlockSpec(memory_space=pltpu.SMEM)
VMEM = pl.BlockSpec(memory_space=pltpu.VMEM)
HBM = pl.BlockSpec(memory_space=pltpu.HBM)
ANY = pl.BlockSpec(memory_space=pl.ANY)


def prep(pat, basis):
    return pl.pallas_call(
        prep_kernel,
        out_shape=CHUNKS,
        in_specs=[SMEM, HBM],
        out_specs=(VMEM,) * len(CHUNKS),
        scratch_shapes=[
            pltpu.VMEM((LA, ROWS, NAO), BF16),
            pltpu.VMEM((NAO // LANES, LA * ROWS, LANES), F32),
            pltpu.SemaphoreType.DMA((LA // 8,)),
        ],
        compiler_params=pltpu.CompilerParams(vmem_limit_bytes=54 * MIB),
        cost_estimate=pl.CostEstimate(flops=10**6, bytes_accessed=3 * 10**6, transcendentals=0),
        name="prep",
    )(pat, basis)


STEPQ = 8


def product_kernel(pat_ref, gpat_ref, basis_ref, occ_ref, vir_ref, *refs):
    out_refs, (first, held, occ, vir, masks) = refs[:-5], refs[-5:]
    i = pl.program_id(0)
    z, y, r = places()
    place = z * NY + y
    b0 = (place * LA) // ABLOCK
    nblocks = pat_ref.shape[2]

    @pl.when(i == 0)
    def _():
        for mb in range(NB):
            rows = pl.ds(mb * BLOCK, BLOCK)
            g = row_mask(lambda n: gpat_ref[mb, n]).astype(BF16)
            vir[rows, :] = vir_ref[rows, :] * g
            for k in range(2):
                b = jnp.minimum(b0 + k, nblocks - 1)
                m = row_mask(lambda n: pat_ref[mb, n, b])
                masks[k, rows, :] = jnp.broadcast_to(m, (BLOCK, NAO)).astype(BF16)
        for jo in range(ROWS // 16):
            start = pl.multiple_of(r * ROWS + 16 * jo, 16)
            g = row_mask(lambda n: gpat_ref[start // BLOCK, n]).astype(BF16)
            occ[pl.ds(16 * jo, 16), :] = occ_ref[pl.ds(start, 16), :] * g

    which = (place * LA + STEPQ * i) // ABLOCK - b0
    mask = masks[which]
    rows_r = occ[...]
    for q in range(STEPQ):
        masked = basis_ref[q] * mask
        f = jnp.dot(rows_r, masked, preferred_element_type=F32).astype(BF16)
        first[pl.ds(pl.multiple_of((STEPQ * i + q) * ROWS, 16), ROWS), :] = f

    @pl.when(i == LA // STEPQ - 1)
    def _():
        v = vir[...]
        n = LA * ROWS // 4
        for t in range(4):
            part = jnp.dot(first[pl.ds(t * n, n), :], v, preferred_element_type=F32)
            for u in range(NAO // LANES):
                held[u, pl.ds(t * n, n), :] = part[:, LANES * u : LANES * (u + 1)]
        emit(z, held, *out_refs)


def products(pat, gpat, basis, occ, vir):
    return pl.pallas_call(
        product_kernel,
        out_shape=WHOLE,
        grid=(LA // STEPQ,),
        in_specs=[
            SMEM,
            SMEM,
            pl.BlockSpec((STEPQ, NAO, NAO), lambda i: (i, 0, 0)),
            pl.BlockSpec((NAO, NAO), lambda i: (0, 0)),
            pl.BlockSpec((NAO, NAO), lambda i: (0, 0)),
        ],
        out_specs=tuple(pl.BlockSpec(c.shape, lambda i: (0, 0, 0)) for c in WHOLE),
        scratch_shapes=[
            pltpu.VMEM((LA * ROWS, NAO), BF16),
            pltpu.VMEM((NAO // LANES, LA * ROWS, LANES), F32),
            pltpu.VMEM((ROWS, NAO), BF16),
            pltpu.VMEM((NAO, NAO), BF16),
            pltpu.VMEM((2, NAO, NAO), BF16),
        ],
        compiler_params=pltpu.CompilerParams(vmem_limit_bytes=56 * MIB),
        cost_estimate=pl.CostEstimate(
            flops=4 * LA * ROWS * NAO * NAO, bytes_accessed=14 * 10**6, transcendentals=0
        ),
        name="products",
    )(pat, gpat, basis, occ, vir)


def shift(value, by, axis, n):
    return lax.ppermute(value, axis, [(i, (i + by) % n) for i in range(n)])


def after(value, *others):
    return lax.optimization_barrier((value,) + others)[0]


GROUPS = ((0, 1, 7), (2, 6, 3, 5, 4))
EORDER = (0, 1, 3, 2)


def both(plus, minus, hops=1):
    return shift(plus, hops, "z", NZ), shift(minus, -hops, "z", NZ)


def round_y(group):
    return shift(group, 1, "y", NY), shift(group, -1, "y", NY)


def far_y(below, above):
    pairs = [(NC * y + c, NC * ((y + 1 - 2 * c) % NY) + c) for y in range(NY) for c in range(NC)]
    value = jnp.where(lax.axis_index("core") == 0, below, above)
    return lax.ppermute(value, ("y", "core"), pairs)


tie = lax.optimization_barrier


def spread(chunks, products_of):
    own, plus, minus, up, down = chunks
    p1, m1 = both(plus, minus)
    up, down = both(up, down, 2)
    pown, pplus, pminus = products_of()
    n1 = jnp.concatenate([own, p1[:2], m1[:2]], axis=0)
    p1 = jnp.concatenate([p1[2:], up], axis=0)
    m1 = jnp.concatenate([m1[2:], down], axis=0)
    p1, m1, n1, pplus, pminus = tie((p1, m1, n1, pplus, pminus))
    p2, m2 = both(p1, m1)
    b1, a1 = round_y(n1)
    p2, m2, b1, a1, pplus, pminus = tie((p2, m2, b1, a1, pplus, pminus))
    p3, m3 = both(p2[2:], m2[2:])
    f1 = far_y(b1, a1)
    q1, r1 = both(pplus, pminus)
    n2 = jnp.concatenate([p2[:2], m2[:2], p3[:2], m3[:2], p3[2:], m3[2:]], axis=0)
    n2, f1 = tie((n2, f1))
    b2, a2 = round_y(n2)
    q2, r2 = both(q1[2:], r1[2:])
    b2, a2, q2, r2 = tie((b2, a2, q2, r2))
    f2 = far_y(b2, a2)
    q3, r3 = both(q2[2:4], r2[2:4])
    q4, r4 = both(q2[4:], r2[4:], 2)
    return [n1, b1, a1, f1, n2, b2, a2, f2], [pown, q1, q2, q3, q4, r4, r3, r2, r1]


ORDER = [(d, e) for group in GROUPS for e in EORDER for d in group]


TILE = 256


def contract_kernel(np_, *refs):
    products_, arrays, (keep_ref, send_ref, left, right) = refs[:np_], refs[np_:-4], refs[-4:]
    z, c = lax.axis_index("z"), lax.axis_index("core")
    first = lax.rem(z + c, 2) == 0
    at = 0
    for a in products_:
        for i in range(min(a.shape[0], 2)):
            left[at % 2, pl.ds(at // 2 * LA, LA), :] = a[i]
            at += 1
    at = 0
    for a in arrays:
        for i in range(a.shape[0]):
            right[at % 2, pl.ds(at // 2 * LA, LA), :] = a[i]
            at += 1
    for t in range(NZ * NY * LA // TILE):
        cols = pl.ds(t * TILE, TILE)
        acc = jnp.zeros((NZ * LA, TILE), F32)
        for h in range(2):
            acc += lax.dot_general(
                left[h], right[h, cols, :], (((1,), (1,)), ((), ())), preferred_element_type=F32
            )
        part = acc.reshape(NZ, LA, TILE)
        for d in range(0, NZ, 2):
            at_a, at_b = (lax.rem(z - d - i + NZ, NZ) // 2 for i in range(2))
            keep_ref[jnp.where(first, at_a, at_b), :, cols] = jnp.where(first, part[d], part[d + 1])
            send_ref[jnp.where(first, at_b, at_a), :, cols] = jnp.where(first, part[d + 1], part[d])


def contract(m, p):
    return pl.pallas_call(
        functools.partial(contract_kernel, len(p)),
        out_shape=(jax.ShapeDtypeStruct((NX, LA, NZ * NY * LA), F32),) * 2,
        in_specs=[VMEM] * (len(p) + len(m)),
        out_specs=(VMEM, VMEM),
        scratch_shapes=[
            pltpu.VMEM((2, NZ * LA, HALF), BF16),
            pltpu.VMEM((2, NZ * NY * LA, HALF), BF16),
        ],
        compiler_params=pltpu.CompilerParams(vmem_limit_bytes=16 * MIB),
        cost_estimate=pl.CostEstimate(
            flops=4 * 320 * 1280 * 1152, bytes_accessed=10**7, transcendentals=0
        ),
        name="contract",
    )(*p, *m)


def pack_kernel(in_ref, out_ref):
    z, y, _ = places()
    total = in_ref[0].astype(F32)
    for k in range(1, NX):
        total += in_ref[k].astype(F32)
    for k, (d, e) in enumerate(ORDER):
        part = total[:, k * LA : (k + 1) * LA]
        oct8 = [part[8 * o : 8 * o + 8] for o in range(5)]
        upper = jnp.concatenate([oct8[0], oct8[1], oct8[2], jnp.zeros((8, 8), F32)], axis=1)
        lower = jnp.concatenate([oct8[3], oct8[4], jnp.zeros((8, 48), F32)], axis=1)
        dest = lax.rem(z - d + NZ, NZ) * NY + lax.rem(y - e + NY, NY)
        out_ref[dest, 0:8, :] = upper
        out_ref[dest, 8:16, :] = lower


def pack(value):
    return pl.pallas_call(
        pack_kernel,
        out_shape=jax.ShapeDtypeStruct((NZ * NY, 16, LANES), F32),
        in_specs=[VMEM],
        out_specs=VMEM,
        name="pack",
    )(value)


def finish_kernel(in_ref, out_ref):
    parts = []
    for y in range(NY):
        total = in_ref[y]
        for z in range(1, NZ):
            total = total + in_ref[z * NY + y]
        for o in range(5):
            lo = (o % 3) * LA
            parts.append(total[8 * (o // 3) : 8 * (o // 3) + 8, lo : lo + LA])
    rows = jnp.concatenate(parts, axis=0)
    rows = jnp.concatenate([rows, jnp.zeros((NY * LA, LANES - LA), F32)], axis=1)
    rows = jnp.concatenate([rows, jnp.zeros((256 - NY * LA, LANES), F32)], axis=0)
    out_ref[...] = rows.T[:LA, : NY * LA] * (1.0 / NAO)


def finish(value):
    return pl.pallas_call(
        finish_kernel,
        out_shape=jax.ShapeDtypeStruct((LA, NY * LA), F32),
        in_specs=[VMEM],
        out_specs=VMEM,
        name="finish",
    )(value)


def local(basis, aux_pattern, green_pattern, green_occ, green_vir):
    pat = jnp.transpose(aux_pattern, (1, 2, 0))
    m, p = spread(
        prep(pat, basis), lambda: products(pat, green_pattern, basis, green_occ, green_vir)
    )
    keep, send = contract(m, p)
    parts = (keep + shift(send, 1, "core", NC)).astype(BF16)
    by_x = lax.all_to_all(parts, "x", split_axis=0, concat_axis=0, tiled=True)
    by_zy = lax.all_to_all(pack(by_x), ("z", "y"), split_axis=0, concat_axis=0, tiled=True)
    return finish(by_zy)


def solution(mesh):
    fine = Mesh(mesh.devices.reshape(NZ, NY, NX, NC), ("z", "y", "x", "core"))
    return jax.shard_map(
        local,
        mesh=fine,
        in_specs=(P(("z", "y"), None, None), P(), P(), P(), P()),
        out_specs=P(("z", "y"), ("x", "core")),
        check_vma=False,
    )
```

```python
import functools

import jax
import jax.numpy as jnp
from jax import lax
from jax.experimental import pallas as pl
from jax.experimental.pallas import tpu as pltpu
from jax.sharding import Mesh, PartitionSpec as P

BLOCK = 64
ABLOCK = 64
NZ, NY, NX, NC = 8, 4, 4, 2
NR = NX * NC
LA = 40
NAO = 384
LANES = 128
ROWS = NAO // NR
SUB = ROWS // NZ
FULL = SUB * NAO
HALF = FULL // 2
NB = NAO // BLOCK
F32 = jnp.float32
BF16 = jnp.bfloat16
MIB = 1024 * 1024


def places():
    z, y, x, c = (lax.axis_index(a) for a in ("z", "y", "x", "core"))
    return z, y, x * NC + c


def row_mask(read):
    lane = lax.broadcasted_iota(jnp.int32, (1, NAO), 1) // BLOCK
    out = jnp.zeros((1, NAO), F32)
    for n in range(NB):
        out = jnp.where(lane == n, read(n).astype(F32), out)
    return out


def emit(z, held, own_ref, plus_ref, minus_ref, *far_refs):
    for d in range(NZ):
        dest = lax.rem(z + d, NZ)
        for j in range(SUB):
            h = j // 3
            if d == 0:
                out_ref, place = own_ref, h
            elif d < 4:
                out_ref, place = plus_ref, 2 * (d - 1) + h
            elif d > 4:
                out_ref, place = minus_ref, 2 * (7 - d) + h
            else:
                out_ref, place = (far_refs[h], 0) if far_refs else ((plus_ref, minus_ref)[h], 6)
            for t in range(NAO // LANES):
                rows = held[t, pl.ds(dest * SUB + j, LA, stride=ROWS), :]
                out_ref[place, :, pl.ds((j % 3) * NAO + LANES * t, LANES)] = rows.astype(BF16)


CHUNKS = tuple(jax.ShapeDtypeStruct((n, LA, HALF), BF16) for n in (2, 6, 6, 1, 1))
WHOLE = tuple(jax.ShapeDtypeStruct((n, LA, HALF), BF16) for n in (2, 7, 7))


def prep_kernel(pat_ref, basis_ref, *refs):
    out_refs, (slab, held, sems) = refs[:-3], refs[-3:]
    z, y, r = places()
    place = z * NY + y
    steps = LA // 8
    start = pl.multiple_of(r * ROWS, 16)
    copies = [
        pltpu.make_async_copy(
            basis_ref.at[pl.ds(8 * o, 8), pl.ds(start, ROWS), :], slab.at[pl.ds(8 * o, 8)], sems.at[o]
        )
        for o in range(steps)
    ]
    for copy in copies:
        copy.start()
    for o in range(steps):
        b = (place * LA + 8 * o) // ABLOCK
        masks = [
            row_mask(lambda n: pat_ref[(r * ROWS + 8 * jo) // BLOCK, n, b]) for jo in range(ROWS // 8)
        ]
        copies[o].wait()
        for jo in range(ROWS // 8):
            for p in range(8 * o, 8 * o + 8):
                rows = slab[p, pl.ds(8 * jo, 8), :].astype(F32) * masks[jo]
                for t in range(NAO // LANES):
                    held[t, pl.ds(p * ROWS + 8 * jo, 8), :] = rows[:, LANES * t : LANES * (t + 1)]
    emit(z, held, *out_refs)


SMEM = pl.BlockSpec(memory_space=pltpu.SMEM)
VMEM = pl.BlockSpec(memory_space=pltpu.VMEM)
HBM = pl.BlockSpec(memory_space=pltpu.HBM)
ANY = pl.BlockSpec(memory_space=pl.ANY)


def prep(pat, basis):
    return pl.pallas_call(
        prep_kernel,
        out_shape=CHUNKS,
        in_specs=[SMEM, HBM],
        out_specs=(VMEM,) * len(CHUNKS),
        scratch_shapes=[
            pltpu.VMEM((LA, ROWS, NAO), BF16),
            pltpu.VMEM((NAO // LANES, LA * ROWS, LANES), F32),
            pltpu.SemaphoreType.DMA((LA // 8,)),
        ],
        compiler_params=pltpu.CompilerParams(vmem_limit_bytes=54 * MIB),
        cost_estimate=pl.CostEstimate(flops=10**6, bytes_accessed=3 * 10**6, transcendentals=0),
        name="prep",
    )(pat, basis)


STEPQ = 8


def product_kernel(pat_ref, gpat_ref, basis_ref, occ_ref, vir_ref, *refs):
    out_refs, (first, held, occ, vir, masks) = refs[:-5], refs[-5:]
    i = pl.program_id(0)
    z, y, r = places()
    place = z * NY + y
    b0 = (place * LA) // ABLOCK
    nblocks = pat_ref.shape[2]

    @pl.when(i == 0)
    def _():
        for mb in range(NB):
            rows = pl.ds(mb * BLOCK, BLOCK)
            g = row_mask(lambda n: gpat_ref[mb, n]).astype(BF16)
            vir[rows, :] = vir_ref[rows, :] * g
            for k in range(2):
                b = jnp.minimum(b0 + k, nblocks - 1)
                m = row_mask(lambda n: pat_ref[mb, n, b])
                masks[k, rows, :] = jnp.broadcast_to(m, (BLOCK, NAO)).astype(BF16)
        for jo in range(ROWS // 16):
            start = pl.multiple_of(r * ROWS + 16 * jo, 16)
            g = row_mask(lambda n: gpat_ref[start // BLOCK, n]).astype(BF16)
            occ[pl.ds(16 * jo, 16), :] = occ_ref[pl.ds(start, 16), :] * g

    which = (place * LA + STEPQ * i) // ABLOCK - b0
    mask = masks[which]
    rows_r = occ[...]
    for q in range(STEPQ):
        masked = basis_ref[q] * mask
        f = jnp.dot(rows_r, masked, preferred_element_type=F32).astype(BF16)
        first[pl.ds(pl.multiple_of((STEPQ * i + q) * ROWS, 16), ROWS), :] = f

    @pl.when(i == LA // STEPQ - 1)
    def _():
        v = vir[...]
        n = LA * ROWS // 4
        for t in range(4):
            part = jnp.dot(first[pl.ds(t * n, n), :], v, preferred_element_type=F32)
            for u in range(NAO // LANES):
                held[u, pl.ds(t * n, n), :] = part[:, LANES * u : LANES * (u + 1)]
        emit(z, held, *out_refs)


def products(pat, gpat, basis, occ, vir):
    return pl.pallas_call(
        product_kernel,
        out_shape=WHOLE,
        grid=(LA // STEPQ,),
        in_specs=[
            SMEM,
            SMEM,
            pl.BlockSpec((STEPQ, NAO, NAO), lambda i: (i, 0, 0)),
            pl.BlockSpec((NAO, NAO), lambda i: (0, 0)),
            pl.BlockSpec((NAO, NAO), lambda i: (0, 0)),
        ],
        out_specs=tuple(pl.BlockSpec(c.shape, lambda i: (0, 0, 0)) for c in WHOLE),
        scratch_shapes=[
            pltpu.VMEM((LA * ROWS, NAO), BF16),
            pltpu.VMEM((NAO // LANES, LA * ROWS, LANES), F32),
            pltpu.VMEM((ROWS, NAO), BF16),
            pltpu.VMEM((NAO, NAO), BF16),
            pltpu.VMEM((2, NAO, NAO), BF16),
        ],
        compiler_params=pltpu.CompilerParams(vmem_limit_bytes=56 * MIB),
        cost_estimate=pl.CostEstimate(
            flops=4 * LA * ROWS * NAO * NAO, bytes_accessed=14 * 10**6, transcendentals=0
        ),
        name="products",
    )(pat, gpat, basis, occ, vir)


def shift(value, by, axis, n):
    return lax.ppermute(value, axis, [(i, (i + by) % n) for i in range(n)])


def after(value, *others):
    return lax.optimization_barrier((value,) + others)[0]


GROUPS = ((0, 1, 7), (2, 6, 3, 5, 4))
EORDER = (0, 1, 3, 2)


def both(plus, minus, hops=1):
    return shift(plus, hops, "z", NZ), shift(minus, -hops, "z", NZ)


def round_y(group):
    return shift(group, 1, "y", NY), shift(group, -1, "y", NY)


def far_y(below, above):
    pairs = [(NC * y + c, NC * ((y + 1 - 2 * c) % NY) + c) for y in range(NY) for c in range(NC)]
    value = jnp.where(lax.axis_index("core") == 0, below, above)
    return lax.ppermute(value, ("y", "core"), pairs)


tie = lax.optimization_barrier


def spread(chunks, products_of):
    own, plus, minus, up, down = chunks
    p1, m1 = both(plus, minus)
    up, down = both(up, down, 2)
    pown, pplus, pminus = products_of()
    n1, k1 = p1[:2], m1[:2]
    p1 = jnp.concatenate([p1[2:], up], axis=0)
    m1 = jnp.concatenate([m1[2:], down], axis=0)
    p1, m1, own, n1, k1, pplus, pminus = tie((p1, m1, own, n1, k1, pplus, pminus))
    n1 = jnp.concatenate([own, n1, k1], axis=0)
    p2, m2 = both(p1, m1)
    b1, a1 = round_y(n1)
    p2, m2, pplus, pminus = tie((p2, m2, pplus, pminus))
    p3, m3 = both(p2[2:], m2[2:])
    f1 = far_y(b1, a1)
    q1, r1 = both(pplus, pminus)
    n2 = jnp.concatenate([p2[:2], m2[:2], p3[:2], m3[:2], p3[2:], m3[2:]], axis=0)
    b2, a2 = round_y(n2)
    q1, r1, f1 = tie((q1, r1, f1))
    q2, r2 = both(q1[2:], r1[2:])
    b2, a2, q2, r2 = tie((b2, a2, q2, r2))
    f2 = far_y(b2, a2)
    q3, r3 = both(q2[2:4], r2[2:4])
    q4, r4 = both(q2[4:], r2[4:], 2)
    return [n1, b1, a1, f1, n2, b2, a2, f2], [pown, q1, q2, q3, q4, r4, r3, r2, r1]


ORDER = [(d, e) for group in GROUPS for e in EORDER for d in group]


TILE = 256


def contract_kernel(np_, *refs):
    products_, arrays, (keep_ref, send_ref, left, right) = refs[:np_], refs[np_:-4], refs[-4:]
    z, c = lax.axis_index("z"), lax.axis_index("core")
    first = lax.rem(z + c, 2) == 0
    at = 0
    for a in products_:
        for i in range(min(a.shape[0], 2)):
            left[at % 2, pl.ds(at // 2 * LA, LA), :] = a[i]
            at += 1
    at = 0
    for a in arrays:
        for i in range(a.shape[0]):
            right[at % 2, pl.ds(at // 2 * LA, LA), :] = a[i]
            at += 1
    for t in range(NZ * NY * LA // TILE):
        cols = pl.ds(t * TILE, TILE)
        acc = jnp.zeros((NZ * LA, TILE), F32)
        for h in range(2):
            acc += lax.dot_general(
                left[h], right[h, cols, :], (((1,), (1,)), ((), ())), preferred_element_type=F32
            )
        part = acc.reshape(NZ, LA, TILE)
        for d in range(0, NZ, 2):
            at_a, at_b = (lax.rem(z - d - i + NZ, NZ) // 2 for i in range(2))
            keep_ref[jnp.where(first, at_a, at_b), :, cols] = jnp.where(first, part[d], part[d + 1])
            send_ref[jnp.where(first, at_b, at_a), :, cols] = jnp.where(first, part[d + 1], part[d])


def contract(m, p):
    return pl.pallas_call(
        functools.partial(contract_kernel, len(p)),
        out_shape=(jax.ShapeDtypeStruct((NX, LA, NZ * NY * LA), F32),) * 2,
        in_specs=[VMEM] * (len(p) + len(m)),
        out_specs=(VMEM, VMEM),
        scratch_shapes=[
            pltpu.VMEM((2, NZ * LA, HALF), BF16),
            pltpu.VMEM((2, NZ * NY * LA, HALF), BF16),
        ],
        compiler_params=pltpu.CompilerParams(vmem_limit_bytes=16 * MIB),
        cost_estimate=pl.CostEstimate(
            flops=4 * 320 * 1280 * 1152, bytes_accessed=10**7, transcendentals=0
        ),
        name="contract",
    )(*p, *m)


def pack_kernel(in_ref, out_ref):
    z, y, _ = places()
    total = in_ref[0].astype(F32)
    for k in range(1, NX):
        total += in_ref[k].astype(F32)
    for k, (d, e) in enumerate(ORDER):
        part = total[:, k * LA : (k + 1) * LA]
        oct8 = [part[8 * o : 8 * o + 8] for o in range(5)]
        upper = jnp.concatenate([oct8[0], oct8[1], oct8[2], jnp.zeros((8, 8), F32)], axis=1)
        lower = jnp.concatenate([oct8[3], oct8[4], jnp.zeros((8, 48), F32)], axis=1)
        dest = lax.rem(z - d + NZ, NZ) * NY + lax.rem(y - e + NY, NY)
        out_ref[dest, 0:8, :] = upper
        out_ref[dest, 8:16, :] = lower


def pack(value):
    return pl.pallas_call(
        pack_kernel,
        out_shape=jax.ShapeDtypeStruct((NZ * NY, 16, LANES), F32),
        in_specs=[VMEM],
        out_specs=VMEM,
        name="pack",
    )(value)


def finish_kernel(in_ref, out_ref):
    parts = []
    for y in range(NY):
        total = in_ref[y]
        for z in range(1, NZ):
            total = total + in_ref[z * NY + y]
        for o in range(5):
            lo = (o % 3) * LA
            parts.append(total[8 * (o // 3) : 8 * (o // 3) + 8, lo : lo + LA])
    rows = jnp.concatenate(parts, axis=0)
    rows = jnp.concatenate([rows, jnp.zeros((NY * LA, LANES - LA), F32)], axis=1)
    rows = jnp.concatenate([rows, jnp.zeros((256 - NY * LA, LANES), F32)], axis=0)
    out_ref[...] = rows.T[:LA, : NY * LA] * (1.0 / NAO)


def finish(value):
    return pl.pallas_call(
        finish_kernel,
        out_shape=jax.ShapeDtypeStruct((LA, NY * LA), F32),
        in_specs=[VMEM],
        out_specs=VMEM,
        name="finish",
    )(value)


def local(basis, aux_pattern, green_pattern, green_occ, green_vir):
    pat = jnp.transpose(aux_pattern, (1, 2, 0))
    m, p = spread(
        prep(pat, basis), lambda: products(pat, green_pattern, basis, green_occ, green_vir)
    )
    keep, send = contract(m, p)
    parts = (keep + shift(send, 1, "core", NC)).astype(BF16)
    by_x = lax.all_to_all(parts, "x", split_axis=0, concat_axis=0, tiled=True)
    by_zy = lax.all_to_all(pack(by_x), ("z", "y"), split_axis=0, concat_axis=0, tiled=True)
    return finish(by_zy)


def solution(mesh):
    fine = Mesh(mesh.devices.reshape(NZ, NY, NX, NC), ("z", "y", "x", "core"))
    return jax.shard_map(
        local,
        mesh=fine,
        in_specs=(P(("z", "y"), None, None), P(), P(), P(), P()),
        out_specs=P(("z", "y"), ("x", "core")),
        check_vma=False,
    )
```

```python
import functools

import jax
import jax.numpy as jnp
from jax import lax
from jax.experimental import pallas as pl
from jax.experimental.pallas import tpu as pltpu
from jax.sharding import Mesh, PartitionSpec as P

BLOCK = 64
ABLOCK = 64
NZ, NY, NX, NC = 8, 4, 4, 2
NR = NX * NC
LA = 40
NAO = 384
LANES = 128
ROWS = NAO // NR
SUB = ROWS // NZ
FULL = SUB * NAO
HALF = FULL // 2
NB = NAO // BLOCK
F32 = jnp.float32
BF16 = jnp.bfloat16
MIB = 1024 * 1024


def places():
    z, y, x, c = (lax.axis_index(a) for a in ("z", "y", "x", "core"))
    return z, y, x * NC + c


def row_mask(read):
    lane = lax.broadcasted_iota(jnp.int32, (1, NAO), 1) // BLOCK
    out = jnp.zeros((1, NAO), F32)
    for n in range(NB):
        out = jnp.where(lane == n, read(n).astype(F32), out)
    return out


def emit(z, held, own_ref, plus_ref, minus_ref, *far_refs):
    for d in range(NZ):
        dest = lax.rem(z + d, NZ)
        for j in range(SUB):
            h = j // 3
            if d == 0:
                out_ref, place = own_ref, h
            elif d < 4:
                out_ref, place = plus_ref, 2 * (d - 1) + h
            elif d > 4:
                out_ref, place = minus_ref, 2 * (7 - d) + h
            else:
                out_ref, place = (far_refs[h], 0) if far_refs else ((plus_ref, minus_ref)[h], 6)
            for t in range(NAO // LANES):
                rows = held[t, pl.ds(dest * SUB + j, LA, stride=ROWS), :]
                out_ref[place, :, pl.ds((j % 3) * NAO + LANES * t, LANES)] = rows.astype(BF16)


CHUNKS = tuple(jax.ShapeDtypeStruct((n, LA, HALF), BF16) for n in (2, 6, 6, 1, 1))
WHOLE = tuple(jax.ShapeDtypeStruct((n, LA, HALF), BF16) for n in (2, 7, 7))


def prep_kernel(pat_ref, basis_ref, *refs):
    out_refs, (slab, held, sems) = refs[:-3], refs[-3:]
    z, y, r = places()
    place = z * NY + y
    steps = LA // 8
    start = pl.multiple_of(r * ROWS, 16)
    copies = [
        pltpu.make_async_copy(
            basis_ref.at[pl.ds(8 * o, 8), pl.ds(start, ROWS), :], slab.at[pl.ds(8 * o, 8)], sems.at[o]
        )
        for o in range(steps)
    ]
    for copy in copies:
        copy.start()
    for o in range(steps):
        b = (place * LA + 8 * o) // ABLOCK
        masks = [
            row_mask(lambda n: pat_ref[(r * ROWS + 8 * jo) // BLOCK, n, b]) for jo in range(ROWS // 8)
        ]
        copies[o].wait()
        for jo in range(ROWS // 8):
            for p in range(8 * o, 8 * o + 8):
                rows = slab[p, pl.ds(8 * jo, 8), :].astype(F32) * masks[jo]
                for t in range(NAO // LANES):
                    held[t, pl.ds(p * ROWS + 8 * jo, 8), :] = rows[:, LANES * t : LANES * (t + 1)]
    emit(z, held, *out_refs)


SMEM = pl.BlockSpec(memory_space=pltpu.SMEM)
VMEM = pl.BlockSpec(memory_space=pltpu.VMEM)
HBM = pl.BlockSpec(memory_space=pltpu.HBM)
ANY = pl.BlockSpec(memory_space=pl.ANY)


def prep(pat, basis):
    return pl.pallas_call(
        prep_kernel,
        out_shape=CHUNKS,
        in_specs=[SMEM, HBM],
        out_specs=(VMEM,) * len(CHUNKS),
        scratch_shapes=[
            pltpu.VMEM((LA, ROWS, NAO), BF16),
            pltpu.VMEM((NAO // LANES, LA * ROWS, LANES), F32),
            pltpu.SemaphoreType.DMA((LA // 8,)),
        ],
        compiler_params=pltpu.CompilerParams(vmem_limit_bytes=54 * MIB),
        cost_estimate=pl.CostEstimate(flops=10**6, bytes_accessed=3 * 10**6, transcendentals=0),
        name="prep",
    )(pat, basis)


STEPQ = 8


def product_kernel(pat_ref, gpat_ref, basis_ref, occ_ref, vir_ref, *refs):
    out_refs, (first, held, occ, vir, masks) = refs[:-5], refs[-5:]
    i = pl.program_id(0)
    z, y, r = places()
    place = z * NY + y
    b0 = (place * LA) // ABLOCK
    nblocks = pat_ref.shape[2]

    @pl.when(i == 0)
    def _():
        for mb in range(NB):
            rows = pl.ds(mb * BLOCK, BLOCK)
            g = row_mask(lambda n: gpat_ref[mb, n]).astype(BF16)
            vir[rows, :] = vir_ref[rows, :] * g
            for k in range(2):
                b = jnp.minimum(b0 + k, nblocks - 1)
                m = row_mask(lambda n: pat_ref[mb, n, b])
                masks[k, rows, :] = jnp.broadcast_to(m, (BLOCK, NAO)).astype(BF16)
        for jo in range(ROWS // 16):
            start = pl.multiple_of(r * ROWS + 16 * jo, 16)
            g = row_mask(lambda n: gpat_ref[start // BLOCK, n]).astype(BF16)
            occ[pl.ds(16 * jo, 16), :] = occ_ref[pl.ds(start, 16), :] * g

    which = (place * LA + STEPQ * i) // ABLOCK - b0
    mask = masks[which]
    rows_r = occ[...]
    for q in range(STEPQ):
        masked = basis_ref[q] * mask
        f = jnp.dot(rows_r, masked, preferred_element_type=F32).astype(BF16)
        first[pl.ds(pl.multiple_of((STEPQ * i + q) * ROWS, 16), ROWS), :] = f

    @pl.when(i == LA // STEPQ - 1)
    def _():
        v = vir[...]
        n = LA * ROWS // 4
        for t in range(4):
            part = jnp.dot(first[pl.ds(t * n, n), :], v, preferred_element_type=F32)
            for u in range(NAO // LANES):
                held[u, pl.ds(t * n, n), :] = part[:, LANES * u : LANES * (u + 1)]
        emit(z, held, *out_refs)


def products(pat, gpat, basis, occ, vir):
    return pl.pallas_call(
        product_kernel,
        out_shape=WHOLE,
        grid=(LA // STEPQ,),
        in_specs=[
            SMEM,
            SMEM,
            pl.BlockSpec((STEPQ, NAO, NAO), lambda i: (i, 0, 0)),
            pl.BlockSpec((NAO, NAO), lambda i: (0, 0)),
            pl.BlockSpec((NAO, NAO), lambda i: (0, 0)),
        ],
        out_specs=tuple(pl.BlockSpec(c.shape, lambda i: (0, 0, 0)) for c in WHOLE),
        scratch_shapes=[
            pltpu.VMEM((LA * ROWS, NAO), BF16),
            pltpu.VMEM((NAO // LANES, LA * ROWS, LANES), F32),
            pltpu.VMEM((ROWS, NAO), BF16),
            pltpu.VMEM((NAO, NAO), BF16),
            pltpu.VMEM((2, NAO, NAO), BF16),
        ],
        compiler_params=pltpu.CompilerParams(vmem_limit_bytes=56 * MIB),
        cost_estimate=pl.CostEstimate(
            flops=4 * LA * ROWS * NAO * NAO, bytes_accessed=14 * 10**6, transcendentals=0
        ),
        name="products",
    )(pat, gpat, basis, occ, vir)


def shift(value, by, axis, n):
    return lax.ppermute(value, axis, [(i, (i + by) % n) for i in range(n)])


def after(value, *others):
    return lax.optimization_barrier((value,) + others)[0]


GROUPS = ((0, 1, 7), (2, 6, 3, 5, 4))
EORDER = (0, 1, 3, 2)


def both(plus, minus, hops=1):
    return shift(plus, hops, "z", NZ), shift(minus, -hops, "z", NZ)


def round_y(group):
    return shift(group, 1, "y", NY), shift(group, -1, "y", NY)


def far_y(below, above):
    pairs = [(NC * y + c, NC * ((y + 1 - 2 * c) % NY) + c) for y in range(NY) for c in range(NC)]
    value = jnp.where(lax.axis_index("core") == 0, below, above)
    return lax.ppermute(value, ("y", "core"), pairs)


tie = lax.optimization_barrier


def spread(chunks, products_of):
    own, plus, minus, up, down = chunks
    p1, m1 = both(plus, minus)
    up, down = both(up, down, 2)
    pown, pplus, pminus = products_of()
    n1, k1 = p1[:2], m1[:2]
    p1 = jnp.concatenate([p1[2:], up], axis=0)
    m1 = jnp.concatenate([m1[2:], down], axis=0)
    p1, m1, own, n1, k1, pplus, pminus = tie((p1, m1, own, n1, k1, pplus, pminus))
    n1 = jnp.concatenate([own, n1, k1], axis=0)
    p2, m2 = both(p1, m1)
    b1, a1 = round_y(n1)
    p2, m2, pplus, pminus = tie((p2, m2, pplus, pminus))
    p3, m3 = both(p2[2:], m2[2:])
    f1 = far_y(b1, a1)
    q1, r1 = both(pplus, pminus)
    n2 = jnp.concatenate([p2[:2], m2[:2], p3[:2], m3[:2], p3[2:], m3[2:]], axis=0)
    b2, a2 = round_y(n2)
    q1, r1, f1 = tie((q1, r1, f1))
    q2, r2 = both(q1[2:], r1[2:])
    b2, a2, q2, r2 = tie((b2, a2, q2, r2))
    f2 = far_y(b2, a2)
    q3, r3 = both(q2[2:4], r2[2:4])
    q4, r4 = both(q2[4:], r2[4:], 2)
    return [n1, b1, a1, f1, n2, b2, a2, f2], [pown, q1, q2, q3, q4, r4, r3, r2, r1]


ORDER = [(d, e) for group in GROUPS for e in EORDER for d in group]


TILE = 256


def contract_kernel(np_, *refs):
    products_, arrays, (keep_ref, send_ref, left, right) = refs[:np_], refs[np_:-4], refs[-4:]
    z, c = lax.axis_index("z"), lax.axis_index("core")
    first = lax.rem(z + c, 2) == 0
    at = 0
    for a in products_:
        for i in range(min(a.shape[0], 2)):
            left[at % 2, pl.ds(at // 2 * LA, LA), :] = a[i]
            at += 1
    at = 0
    for a in arrays:
        for i in range(a.shape[0]):
            right[at % 2, pl.ds(at // 2 * LA, LA), :] = a[i]
            at += 1
    for t in range(NZ * NY * LA // TILE):
        cols = pl.ds(t * TILE, TILE)
        acc = jnp.zeros((NZ * LA, TILE), F32)
        for h in range(2):
            acc += lax.dot_general(
                left[h], right[h, cols, :], (((1,), (1,)), ((), ())), preferred_element_type=F32
            )
        part = acc.reshape(NZ, LA, TILE)
        for d in range(0, NZ, 2):
            at_a, at_b = (lax.rem(z - d - i + NZ, NZ) // 2 for i in range(2))
            keep_ref[jnp.where(first, at_a, at_b), :, cols] = jnp.where(first, part[d], part[d + 1])
            send_ref[jnp.where(first, at_b, at_a), :, cols] = jnp.where(first, part[d + 1], part[d])


def contract(m, p):
    return pl.pallas_call(
        functools.partial(contract_kernel, len(p)),
        out_shape=(jax.ShapeDtypeStruct((NX, LA, NZ * NY * LA), F32),) * 2,
        in_specs=[VMEM] * (len(p) + len(m)),
        out_specs=(VMEM, VMEM),
        scratch_shapes=[
            pltpu.VMEM((2, NZ * LA, HALF), BF16),
            pltpu.VMEM((2, NZ * NY * LA, HALF), BF16),
        ],
        compiler_params=pltpu.CompilerParams(vmem_limit_bytes=16 * MIB),
        cost_estimate=pl.CostEstimate(
            flops=4 * 320 * 1280 * 1152, bytes_accessed=10**7, transcendentals=0
        ),
        name="contract",
    )(*p, *m)


def pack_kernel(in_ref, out_ref):
    z, y, _ = places()
    total = in_ref[0].astype(F32)
    for k in range(1, NX):
        total += in_ref[k].astype(F32)
    for k, (d, e) in enumerate(ORDER):
        part = total[:, k * LA : (k + 1) * LA]
        oct8 = [part[8 * o : 8 * o + 8] for o in range(5)]
        upper = jnp.concatenate([oct8[0], oct8[1], oct8[2], jnp.zeros((8, 8), F32)], axis=1)
        lower = jnp.concatenate([oct8[3], oct8[4], jnp.zeros((8, 48), F32)], axis=1)
        dest = lax.rem(z - d + NZ, NZ) * NY + lax.rem(y - e + NY, NY)
        out_ref[dest, 0:8, :] = upper
        out_ref[dest, 8:16, :] = lower


def pack(value):
    return pl.pallas_call(
        pack_kernel,
        out_shape=jax.ShapeDtypeStruct((NZ * NY, 16, LANES), F32),
        in_specs=[VMEM],
        out_specs=VMEM,
        compiler_params=pltpu.CompilerParams(vmem_limit_bytes=8 * MIB),
        name="pack",
    )(value)


def finish_kernel(in_ref, out_ref):
    parts = []
    for y in range(NY):
        total = in_ref[y]
        for z in range(1, NZ):
            total = total + in_ref[z * NY + y]
        for o in range(5):
            lo = (o % 3) * LA
            parts.append(total[8 * (o // 3) : 8 * (o // 3) + 8, lo : lo + LA])
    rows = jnp.concatenate(parts, axis=0)
    rows = jnp.concatenate([rows, jnp.zeros((NY * LA, LANES - LA), F32)], axis=1)
    rows = jnp.concatenate([rows, jnp.zeros((256 - NY * LA, LANES), F32)], axis=0)
    out_ref[...] = rows.T[:LA, : NY * LA] * (1.0 / NAO)


def finish(value):
    return pl.pallas_call(
        finish_kernel,
        out_shape=jax.ShapeDtypeStruct((LA, NY * LA), F32),
        in_specs=[VMEM],
        out_specs=VMEM,
        compiler_params=pltpu.CompilerParams(vmem_limit_bytes=8 * MIB),
        name="finish",
    )(value)


def local(basis, aux_pattern, green_pattern, green_occ, green_vir):
    pat = jnp.transpose(aux_pattern, (1, 2, 0))
    m, p = spread(
        prep(pat, basis), lambda: products(pat, green_pattern, basis, green_occ, green_vir)
    )
    keep, send = contract(m, p)
    parts = (keep + shift(send, 1, "core", NC)).astype(BF16)
    by_x = lax.all_to_all(parts, "x", split_axis=0, concat_axis=0, tiled=True)
    by_zy = lax.all_to_all(pack(by_x), ("z", "y"), split_axis=0, concat_axis=0, tiled=True)
    return finish(by_zy)


def solution(mesh):
    fine = Mesh(mesh.devices.reshape(NZ, NY, NX, NC), ("z", "y", "x", "core"))
    return jax.shard_map(
        local,
        mesh=fine,
        in_specs=(P(("z", "y"), None, None), P(), P(), P(), P()),
        out_specs=P(("z", "y"), ("x", "core")),
        check_vma=False,
    )
```

```python
import functools

import jax
import jax.numpy as jnp
from jax import lax
from jax.experimental import pallas as pl
from jax.experimental.pallas import tpu as pltpu
from jax.sharding import Mesh, PartitionSpec as P

BLOCK = 64
ABLOCK = 64
NZ, NY, NX, NC = 8, 4, 4, 2
NR = NX * NC
LA = 40
NAO = 384
LANES = 128
ROWS = NAO // NR
SUB = ROWS // NZ
FULL = SUB * NAO
HALF = FULL // 2
NB = NAO // BLOCK
F32 = jnp.float32
BF16 = jnp.bfloat16
MIB = 1024 * 1024


def places():
    z, y, x, c = (lax.axis_index(a) for a in ("z", "y", "x", "core"))
    return z, y, x * NC + c


def row_mask(read):
    lane = lax.broadcasted_iota(jnp.int32, (1, NAO), 1) // BLOCK
    out = jnp.zeros((1, NAO), F32)
    for n in range(NB):
        out = jnp.where(lane == n, read(n).astype(F32), out)
    return out


def emit(z, held, own_ref, plus_ref, minus_ref, *far_refs):
    for d in range(NZ):
        dest = lax.rem(z + d, NZ)
        for j in range(SUB):
            h = j // 3
            if d == 0:
                out_ref, place = own_ref, h
            elif d < 4:
                out_ref, place = plus_ref, 2 * (d - 1) + h
            elif d > 4:
                out_ref, place = minus_ref, 2 * (7 - d) + h
            else:
                out_ref, place = (far_refs[h], 0) if far_refs else ((plus_ref, minus_ref)[h], 6)
            for t in range(NAO // LANES):
                rows = held[t, pl.ds(dest * SUB + j, LA, stride=ROWS), :]
                out_ref[place, :, pl.ds((j % 3) * NAO + LANES * t, LANES)] = rows.astype(BF16)


CHUNKS = tuple(jax.ShapeDtypeStruct((n, LA, HALF), BF16) for n in (2, 6, 6, 1, 1))
WHOLE = tuple(jax.ShapeDtypeStruct((n, LA, HALF), BF16) for n in (2, 7, 7))


def prep_kernel(pat_ref, basis_ref, *refs):
    out_refs, (slab, held, sems) = refs[:-3], refs[-3:]
    z, y, r = places()
    place = z * NY + y
    steps = LA // 8
    start = pl.multiple_of(r * ROWS, 16)
    copies = [
        pltpu.make_async_copy(
            basis_ref.at[pl.ds(8 * o, 8), pl.ds(start, ROWS), :], slab.at[pl.ds(8 * o, 8)], sems.at[o]
        )
        for o in range(steps)
    ]
    for copy in copies:
        copy.start()
    for o in range(steps):
        b = (place * LA + 8 * o) // ABLOCK
        masks = [
            row_mask(lambda n: pat_ref[(r * ROWS + 8 * jo) // BLOCK, n, b]) for jo in range(ROWS // 8)
        ]
        copies[o].wait()
        for jo in range(ROWS // 8):
            for p in range(8 * o, 8 * o + 8):
                rows = slab[p, pl.ds(8 * jo, 8), :].astype(F32) * masks[jo]
                for t in range(NAO // LANES):
                    held[t, pl.ds(p * ROWS + 8 * jo, 8), :] = rows[:, LANES * t : LANES * (t + 1)]
    emit(z, held, *out_refs)


SMEM = pl.BlockSpec(memory_space=pltpu.SMEM)
VMEM = pl.BlockSpec(memory_space=pltpu.VMEM)
HBM = pl.BlockSpec(memory_space=pltpu.HBM)
ANY = pl.BlockSpec(memory_space=pl.ANY)


def prep(pat, basis):
    return pl.pallas_call(
        prep_kernel,
        out_shape=CHUNKS,
        in_specs=[SMEM, HBM],
        out_specs=(VMEM,) * len(CHUNKS),
        scratch_shapes=[
            pltpu.VMEM((LA, ROWS, NAO), BF16),
            pltpu.VMEM((NAO // LANES, LA * ROWS, LANES), F32),
            pltpu.SemaphoreType.DMA((LA // 8,)),
        ],
        compiler_params=pltpu.CompilerParams(vmem_limit_bytes=54 * MIB),
        cost_estimate=pl.CostEstimate(flops=10**6, bytes_accessed=3 * 10**6, transcendentals=0),
        name="prep",
    )(pat, basis)


STEPQ = 8


def product_kernel(pat_ref, gpat_ref, basis_ref, occ_ref, vir_ref, *refs):
    out_refs, (first, held, occ, vir, masks) = refs[:-5], refs[-5:]
    i = pl.program_id(0)
    z, y, r = places()
    place = z * NY + y
    b0 = (place * LA) // ABLOCK
    nblocks = pat_ref.shape[2]

    @pl.when(i == 0)
    def _():
        for mb in range(NB):
            rows = pl.ds(mb * BLOCK, BLOCK)
            g = row_mask(lambda n: gpat_ref[mb, n]).astype(BF16)
            vir[rows, :] = vir_ref[rows, :] * g
            for k in range(2):
                b = jnp.minimum(b0 + k, nblocks - 1)
                m = row_mask(lambda n: pat_ref[mb, n, b])
                masks[k, rows, :] = jnp.broadcast_to(m, (BLOCK, NAO)).astype(BF16)
        for jo in range(ROWS // 16):
            start = pl.multiple_of(r * ROWS + 16 * jo, 16)
            g = row_mask(lambda n: gpat_ref[start // BLOCK, n]).astype(BF16)
            occ[pl.ds(16 * jo, 16), :] = occ_ref[pl.ds(start, 16), :] * g

    which = (place * LA + STEPQ * i) // ABLOCK - b0
    mask = masks[which]
    rows_r = occ[...]
    for q in range(STEPQ):
        masked = basis_ref[q] * mask
        f = jnp.dot(rows_r, masked, preferred_element_type=F32).astype(BF16)
        first[pl.ds(pl.multiple_of((STEPQ * i + q) * ROWS, 16), ROWS), :] = f

    @pl.when(i == LA // STEPQ - 1)
    def _():
        v = vir[...]
        n = LA * ROWS // 4
        for t in range(4):
            part = jnp.dot(first[pl.ds(t * n, n), :], v, preferred_element_type=F32)
            for u in range(NAO // LANES):
                held[u, pl.ds(t * n, n), :] = part[:, LANES * u : LANES * (u + 1)]
        emit(z, held, *out_refs)


def products(pat, gpat, basis, occ, vir):
    return pl.pallas_call(
        product_kernel,
        out_shape=WHOLE,
        grid=(LA // STEPQ,),
        in_specs=[
            SMEM,
            SMEM,
            pl.BlockSpec((STEPQ, NAO, NAO), lambda i: (i, 0, 0)),
            pl.BlockSpec((NAO, NAO), lambda i: (0, 0)),
            pl.BlockSpec((NAO, NAO), lambda i: (0, 0)),
        ],
        out_specs=tuple(pl.BlockSpec(c.shape, lambda i: (0, 0, 0)) for c in WHOLE),
        scratch_shapes=[
            pltpu.VMEM((LA * ROWS, NAO), BF16),
            pltpu.VMEM((NAO // LANES, LA * ROWS, LANES), F32),
            pltpu.VMEM((ROWS, NAO), BF16),
            pltpu.VMEM((NAO, NAO), BF16),
            pltpu.VMEM((2, NAO, NAO), BF16),
        ],
        compiler_params=pltpu.CompilerParams(vmem_limit_bytes=56 * MIB),
        cost_estimate=pl.CostEstimate(
            flops=4 * LA * ROWS * NAO * NAO, bytes_accessed=14 * 10**6, transcendentals=0
        ),
        name="products",
    )(pat, gpat, basis, occ, vir)


def shift(value, by, axis, n):
    return lax.ppermute(value, axis, [(i, (i + by) % n) for i in range(n)])


def after(value, *others):
    return lax.optimization_barrier((value,) + others)[0]


GROUPS = ((0, 1, 7), (2, 6, 3, 5, 4))
EORDER = (0, 1, 3, 2)


def both(plus, minus, hops=1):
    return shift(plus, hops, "z", NZ), shift(minus, -hops, "z", NZ)


def round_y(group):
    return shift(group, 1, "y", NY), shift(group, -1, "y", NY)


def far_y(below, above):
    pairs = [(NC * y + c, NC * ((y + 1 - 2 * c) % NY) + c) for y in range(NY) for c in range(NC)]
    value = jnp.where(lax.axis_index("core") == 0, below, above)
    return lax.ppermute(value, ("y", "core"), pairs)


tie = lax.optimization_barrier


def spread(chunks, products_of):
    own, plus, minus, up, down = chunks
    p1, m1 = both(plus, minus)
    up, down = both(up, down, 2)
    pown, pplus, pminus = products_of()
    n1, k1 = p1[:2], m1[:2]
    p1 = jnp.concatenate([p1[2:], up], axis=0)
    m1 = jnp.concatenate([m1[2:], down], axis=0)
    p1, m1, own, n1, k1, pplus, pminus = tie((p1, m1, own, n1, k1, pplus, pminus))
    n1 = jnp.concatenate([own, n1, k1], axis=0)
    p2, m2 = both(p1, m1)
    b1, a1 = round_y(n1)
    p2, m2, pplus, pminus = tie((p2, m2, pplus, pminus))
    p3, m3 = both(p2[2:], m2[2:])
    f1 = far_y(b1, a1)
    q1, r1 = both(pplus, pminus)
    n2 = jnp.concatenate([p2[:2], m2[:2], p3[:2], m3[:2], p3[2:], m3[2:]], axis=0)
    b2, a2 = round_y(n2)
    q1, r1, f1 = tie((q1, r1, f1))
    q2, r2 = both(q1[2:], r1[2:])
    b2, a2, q2, r2 = tie((b2, a2, q2, r2))
    f2 = far_y(b2, a2)
    q3, r3 = both(q2[2:4], r2[2:4])
    q4, r4 = both(q2[4:], r2[4:], 2)
    return [n1, b1, a1, f1, n2, b2, a2, f2], [pown, q1, q2, q3, q4, r4, r3, r2, r1]


ORDER = [(d, e) for group in GROUPS for e in EORDER for d in group]


TILE = 256


def contract_kernel(np_, *refs):
    products_, arrays, (keep_ref, send_ref, left, right) = refs[:np_], refs[np_:-4], refs[-4:]
    z, c = lax.axis_index("z"), lax.axis_index("core")
    first = lax.rem(z + c, 2) == 0
    at = 0
    for a in products_:
        for i in range(min(a.shape[0], 2)):
            left[at % 2, pl.ds(at // 2 * LA, LA), :] = a[i]
            at += 1
    at = 0
    for a in arrays:
        for i in range(a.shape[0]):
            right[at % 2, pl.ds(at // 2 * LA, LA), :] = a[i]
            at += 1
    for t in range(NZ * NY * LA // TILE):
        cols = pl.ds(t * TILE, TILE)
        acc = jnp.zeros((NZ * LA, TILE), F32)
        for h in range(2):
            acc += lax.dot_general(
                left[h], right[h, cols, :], (((1,), (1,)), ((), ())), preferred_element_type=F32
            )
        part = acc.reshape(NZ, LA, TILE)
        for d in range(0, NZ, 2):
            at_a, at_b = (lax.rem(z - d - i + NZ, NZ) // 2 for i in range(2))
            keep_ref[jnp.where(first, at_a, at_b), :, cols] = jnp.where(first, part[d], part[d + 1])
            send_ref[jnp.where(first, at_b, at_a), :, cols] = jnp.where(first, part[d + 1], part[d])


def contract(m, p):
    return pl.pallas_call(
        functools.partial(contract_kernel, len(p)),
        out_shape=(jax.ShapeDtypeStruct((NX, LA, NZ * NY * LA), F32),) * 2,
        in_specs=[VMEM] * (len(p) + len(m)),
        out_specs=(VMEM, VMEM),
        scratch_shapes=[
            pltpu.VMEM((2, NZ * LA, HALF), BF16),
            pltpu.VMEM((2, NZ * NY * LA, HALF), BF16),
        ],
        compiler_params=pltpu.CompilerParams(vmem_limit_bytes=16 * MIB),
        cost_estimate=pl.CostEstimate(
            flops=4 * 320 * 1280 * 1152, bytes_accessed=10**7, transcendentals=0
        ),
        name="contract",
    )(*p, *m)


def pack_kernel(in_ref, out_ref):
    z, y, _ = places()
    total = in_ref[0].astype(F32)
    for k in range(1, NX):
        total += in_ref[k].astype(F32)
    for k, (d, e) in enumerate(ORDER):
        part = total[:, k * LA : (k + 1) * LA]
        oct8 = [part[8 * o : 8 * o + 8] for o in range(5)]
        upper = jnp.concatenate([oct8[0], oct8[1], oct8[2], jnp.zeros((8, 8), F32)], axis=1)
        lower = jnp.concatenate([oct8[3], oct8[4], jnp.zeros((8, 48), F32)], axis=1)
        dest = lax.rem(z - d + NZ, NZ) * NY + lax.rem(y - e + NY, NY)
        out_ref[dest] = jnp.concatenate([upper, lower], axis=0).astype(BF16)


def pack(value):
    return pl.pallas_call(
        pack_kernel,
        out_shape=jax.ShapeDtypeStruct((NZ * NY, 16, LANES), BF16),
        in_specs=[VMEM],
        out_specs=VMEM,
        compiler_params=pltpu.CompilerParams(vmem_limit_bytes=8 * MIB),
        name="pack",
    )(value)


def finish_kernel(in_ref, out_ref):
    parts = []
    for y in range(NY):
        total = in_ref[y].astype(F32)
        for z in range(1, NZ):
            total = total + in_ref[z * NY + y].astype(F32)
        for o in range(5):
            lo = (o % 3) * LA
            parts.append(total[8 * (o // 3) : 8 * (o // 3) + 8, lo : lo + LA])
    rows = jnp.concatenate(parts, axis=0)
    rows = jnp.concatenate([rows, jnp.zeros((NY * LA, LANES - LA), F32)], axis=1)
    rows = jnp.concatenate([rows, jnp.zeros((256 - NY * LA, LANES), F32)], axis=0)
    out_ref[...] = rows.T[:LA, : NY * LA] * (1.0 / NAO)


def finish(value):
    return pl.pallas_call(
        finish_kernel,
        out_shape=jax.ShapeDtypeStruct((LA, NY * LA), F32),
        in_specs=[VMEM],
        out_specs=VMEM,
        compiler_params=pltpu.CompilerParams(vmem_limit_bytes=8 * MIB),
        name="finish",
    )(value)


def local(basis, aux_pattern, green_pattern, green_occ, green_vir):
    pat = jnp.transpose(aux_pattern, (1, 2, 0))
    m, p = spread(
        prep(pat, basis), lambda: products(pat, green_pattern, basis, green_occ, green_vir)
    )
    keep, send = contract(m, p)
    parts = (keep + shift(send, 1, "core", NC)).astype(BF16)
    by_x = lax.all_to_all(parts, "x", split_axis=0, concat_axis=0, tiled=True)
    by_zy = lax.all_to_all(pack(by_x), ("z", "y"), split_axis=0, concat_axis=0, tiled=True)
    return finish(by_zy)


def solution(mesh):
    fine = Mesh(mesh.devices.reshape(NZ, NY, NX, NC), ("z", "y", "x", "core"))
    return jax.shard_map(
        local,
        mesh=fine,
        in_specs=(P(("z", "y"), None, None), P(), P(), P(), P()),
        out_specs=P(("z", "y"), ("x", "core")),
        check_vma=False,
    )
```
